128 devices in a mesh: img: 8 (over z_lo, x), txt: 16 (over z_hi, y, core).
Axes of the slice: x: 4, y: 4, z: 4 (z_hi: 2, z_lo: 2; z = z_hi * 2 + z_lo), core: 2. Of those that a mesh axis runs over, the one named last changes fastest.
Arguments:
- images: bfloat16 [22528, 1152], P(('img', 'txt')), may hold values from -0.19921875 to 0.19921875
- texts: bfloat16 [22528, 1152], P(('txt', 'img')), may hold values from -0.19921875 to 0.19921875
- match: int32 [22528], P(('img', 'txt')), may hold values from 0 to 22527, as said below
- log_scale: float32 [], replicated, may hold values from 2 to 2.8
- bias: float32 [], replicated, may hold values from -11 to -8
Outputs:
- loss: float32 [], replicated
- image_grad: float32 [22528, 1152], P(('img', 'txt'))
- text_grad: float32 [22528, 1152], P(('txt', 'img'))
The draws below stay inside these ranges and needn't reach their ends.
Inputs may be any that keep to these rules, and one draw needn't show every extreme that they name: match names every text exactly once.
All inputs are finite; a program needn't handle non-finite values.
Results may differ from the reference program's by a relative error of at most 0.0044.
Values may be sent and summed in bfloat16 or wider, within the bound.
A program may use at most 128 MiB of HBM per device.

```python
import math
import jax
import jax.numpy as jnp
from jax import lax

D = 1152
BATCH = 22528
IMG_BLOCK = 2816


CLIP_LIMIT = 0.19921875


def shared_parts(key):
    pairing = jax.random.permutation(jax.random.fold_in(key, 101), BATCH).astype(jnp.int32)
    gaussian = jax.random.normal(jax.random.fold_in(key, 102), (BATCH, D), jnp.float32)
    common = jax.random.normal(jax.random.fold_in(key, 103), (D,), jnp.float32)
    phases = jax.random.uniform(jax.random.fold_in(key, 104), (2,), jnp.float32, 0.0, 2.0 * math.pi)
    jitter = jax.random.uniform(jax.random.fold_in(key, 105), (2, BATCH), jnp.float32, 0.5, 1.5)
    position = jnp.arange(BATCH, dtype=jnp.float32) * (2.0 * math.pi / BATCH)
    image_coeff = 0.3 * jitter[0] * jnp.cos(position + phases[0])
    text_coeff = 0.3 * jitter[1] * jnp.cos(position + phases[1])
    image_rows = gaussian + image_coeff[:, None] * common[None, :]
    return (pairing, image_rows, common, text_coeff)


def draw_match(key, part):
    pairing = shared_parts(key)[0]
    return pairing


def draw_images(key, part):
    pairing, image_rows, common, text_coeff = shared_parts(key)
    return jnp.clip(0.03 * image_rows, -CLIP_LIMIT, CLIP_LIMIT).astype(jnp.bfloat16)


def draw_texts(key, part):
    pairing, image_rows, common, text_coeff = shared_parts(key)
    key = jax.random.fold_in(key, 2)
    fresh_noise = jax.random.normal(key, (BATCH, D), jnp.float32)
    paired = 0.7 * image_rows + 0.7 * fresh_noise
    placed = jnp.zeros((BATCH, D), jnp.float32).at[pairing].set(paired)
    text_rows = placed + text_coeff[:, None] * common[None, :]
    return jnp.clip(0.03 * text_rows, -CLIP_LIMIT, CLIP_LIMIT).astype(jnp.bfloat16)


def setup_inputs(seed: int = 0) -> dict:
    key_list = jax.random.split(jax.random.key(seed), 6)
    images = draw_images(jax.random.fold_in(key_list[5], 71), 0)
    texts = draw_texts(jax.random.fold_in(key_list[5], 71), 0)
    match = draw_match(jax.random.fold_in(key_list[5], 71), 0)
    log_scale = jnp.clip(jax.random.uniform(key_list[3], (), jnp.float32, 2.0, 2.8), 2.0, 2.8)
    bias = jnp.clip(jax.random.uniform(key_list[4], (), jnp.float32, -11.0, -8.0), -11.0, -8.0)
    return {"images": images, "texts": texts, "match": match, "log_scale": log_scale, "bias": bias}


EPS = 1e-06

def normalize(rows):
    return rows * lax.rsqrt(lax.optimization_barrier(jnp.sum(rows * rows, axis=-1, keepdims=True)) + EPS)

def reference(images, texts, match, log_scale, bias):
    scale = jnp.exp(log_scale)
    u_full, back_image = jax.vjp(normalize, images.astype(jnp.float32))
    v_full, back_text = jax.vjp(normalize, texts.astype(jnp.float32))
    u_low = u_full.astype(jnp.bfloat16)
    v_low = v_full.astype(jnp.bfloat16)
    block = IMG_BLOCK
    count = BATCH // block
    columns = jnp.arange(BATCH, dtype=jnp.int32)

    def step(carry, index):
        text_acc, loss_acc = carry
        start = (index * block).astype(jnp.int32)
        image_part = lax.dynamic_slice_in_dim(u_low, start, block, 0)
        match_part = lax.dynamic_slice_in_dim(match, start, block, 0)
        logits = scale * jnp.dot(image_part, v_low.T, preferred_element_type=jnp.float32) + bias
        positive = (match_part[:, None] == columns[None, :]).astype(jnp.float32)
        sign = 2.0 * positive - 1.0
        loss_acc = loss_acc + jnp.sum(jax.nn.softplus(-sign * logits))
        grads = (jax.nn.sigmoid(logits) - positive).astype(jnp.bfloat16)
        image_part_grad = scale * jnp.dot(grads, v_low, preferred_element_type=jnp.float32)
        text_acc = text_acc + scale * jnp.dot(grads.T, image_part, preferred_element_type=jnp.float32)
        return ((text_acc, loss_acc), image_part_grad)
    start_carry = (jnp.zeros((BATCH, D), jnp.float32), jnp.zeros((), jnp.float32))
    (text_acc, loss_sum), image_parts = lax.scan(step, start_carry, jnp.arange(count, dtype=jnp.int32))
    image_acc = image_parts.reshape(BATCH, D)
    image_grad = back_image(image_acc)[0]
    text_grad = back_text(text_acc)[0]
    return (loss_sum / BATCH, image_grad, text_grad)
```

```python
import functools

import jax
import jax.numpy as jnp
from jax import lax
from jax.experimental import pallas as pl
from jax.experimental.pallas import tpu as pltpu
from jax.sharding import PartitionSpec as P

EPS = 1e-06
ROWS = 176
D = 1152
HALF = 704
CUT = 96
LOG2E = 1.4426950408889634
LN2 = 0.6931471805599453
BATCH = 22528
MESH = pl.DeviceIdType.MESH
F32 = jnp.float32
BF16 = jnp.bfloat16

ORDER = (7, 5, 6, 4, 1, 2, 3, 0)
PLACE = {k: i for i, k in enumerate(ORDER)}


def other_row(k):
    return 352 * PLACE[k]


def same_row(k):
    return 352 * PLACE[k] + ROWS


def nt(a, b):
    return lax.dot_general(a, b, (((1,), (1,)), ((), ())), preferred_element_type=F32)


def nn(a, b):
    return lax.dot_general(a, b, (((1,), (0,)), ((), ())), preferred_element_type=F32)


def tn(a, b):
    return lax.dot_general(a, b, (((0,), (0,)), ((), ())), preferred_element_type=F32)


def kernel(
    ls_ref, bias_ref, img_ref, txt_ref, lab_ref,
    du_ref, dv_ref, loss_ref,
    u, v, g0, g1, labs, labb, acc, lossbuf,
    dvf, core_out, core_in, stage, recv,
    gs, gr, cs, cr, lsend, lrecv, rs, rr, ccs, ccr, ps, pr,
):
    im = lax.axis_index("img")
    tx = lax.axis_index("txt")
    x = im % 4
    z = (tx // 8) * 2 + im // 4
    y = (tx // 2) % 4
    c = tx % 2

    def dev(dx=0, dy=0, zz=None, dc=0):
        z2 = z if zz is None else zz
        return ((z2 % 2) * 4 + (x + dx) % 4, (z2 // 2) * 8 + ((y + dy) % 4) * 2 + (c + dc) % 2)

    zi = z + 1 - 2 * (z % 2)
    zt = 3 - z
    plus = (dev(dy=1), dev(dx=1))
    minus = (dev(dy=3), dev(dx=3))
    part = (dev(zz=zi), dev(zz=zt))
    core = dev(dc=1)

    group = []
    for dy, dz, k in ((1, 0, 1), (3, 0, 2), (0, 1, 3), (2, 0, 4), (1, 1, 5), (3, 1, 6), (2, 1, 7)):
        for dc in (0, 1):
            group.append((dev(dy=dy, zz=zi if dz else z, dc=dc), 2 * PLACE[k] + 1 - dc))
    group.append((core, 2 * PLACE[0]))

    barrier = pltpu.get_barrier_semaphore()
    partners = [d for d, _ in group] + [plus[1], minus[1], part[1]]
    for d in partners:
        pl.semaphore_signal(barrier, inc=1, device_id=d, device_id_type=MESH)

    def norm(ref):
        rows = ref[...].astype(F32)
        return (rows * lax.rsqrt(jnp.sum(rows * rows, axis=-1, keepdims=True) + EPS)).astype(BF16)

    u[pl.ds(same_row(0), ROWS), :] = norm(img_ref)
    v[pl.ds(0, ROWS), :] = norm(txt_ref)
    labs[2 * PLACE[0] + 1] = lab_ref[...]
    pl.semaphore_wait(barrier, len(partners))

    sent = []

    def copy(src, dst, ss, sr, d):
        return pltpu.make_async_remote_copy(
            src_ref=src, dst_ref=dst, send_sem=ss, recv_sem=sr, device_id=d, device_id_type=MESH
        )

    def start(cp):
        cp.start()
        sent.append(cp)

    def base(f, k):
        return same_row(k) if f == 0 else ROWS * k

    def piece(f, k, lo, n):
        return (u, v)[f].at[pl.ds(base(f, k) + lo, n), :]

    moves = (
        (0, 1, 0, CUT, plus),
        (0, 1, CUT, ROWS - CUT, plus),
        (0, 2, CUT, ROWS - CUT, minus),
        (0, 2, 0, CUT, minus),
        (0, 3, 0, ROWS, part),
        (1, 4, 0, CUT, plus),
        (2, 4, CUT, ROWS - CUT, minus),
        (3, 5, 0, ROWS, plus),
        (3, 6, 0, ROWS, minus),
        (4, 7, 0, CUT, part),
        (4, 7, CUT, ROWS - CUT, part),
    )

    def gcopy(f, i):
        a, b, lo, n, to = moves[i]
        return copy(piece(f, a, lo, n), piece(f, b, lo, n), gs.at[f, i], gr.at[f, i], to[f])

    def gstart(i):
        for f in (0, 1):
            start(gcopy(f, i))

    def gwait(i):
        for f in (0, 1):
            gcopy(f, i).wait_recv()

    def xcopy(k):
        return copy(
            u.at[pl.ds(same_row(k), ROWS), :], u.at[pl.ds(other_row(k), ROWS), :], cs.at[k], cr.at[k], core
        )

    for i in (0, 2, 4, 1, 3):
        gstart(i)
    for n, (d, slot) in enumerate(group):
        start(copy(labs.at[2 * PLACE[0] + 1], labs.at[slot], lsend.at[n], lrecv.at[n], d))
    start(xcopy(0))

    scale = jnp.exp(jnp.full((8, 128), ls_ref[0], F32))
    c1 = scale[0:1, 0:1] * LOG2E
    c0 = jnp.full((1, 1), bias_ref[0] * LOG2E, F32)
    acc[...] = jnp.zeros_like(acc)

    for n, (d, slot) in enumerate(group):
        copy(labs.at[2 * PLACE[0] + 1], labs.at[slot], lsend.at[n], lrecv.at[n], d).wait_recv()
    bases = []
    for dx, zz in ((0, z), (3, z), (1, z), (0, zt), (2, z), (3, zt), (1, zt), (2, zt)):
        i2, t2 = dev(dx=dx, zz=zz)
        bases.append((t2 * 8 + i2) * ROWS)
    for s in range(16):
        lab = labs[s]
        place = jnp.full((8, 128), -1, jnp.int32)
        for j, b in enumerate(bases):
            rel = lab - b
            place = jnp.where((rel >= 0) & (rel < ROWS), rel + ROWS * j, place)
        placef = place.astype(F32)
        first = jnp.broadcast_to(placef[0:1, :], (128, 128)).T
        second = jnp.broadcast_to(placef[1:2, :], (128, 128)).T
        labb[pl.ds(s * ROWS, 128), :] = first
        labb[pl.ds(s * ROWS + 128, 48), :] = second[0:48, :]

    gh = (g0, g1)

    def logits(row, h):
        rows = pl.ds(row, 352)
        s = nt(u[rows, :], v[h * HALF : (h + 1) * HALF, :])
        l2 = s * c1 + c0
        e = jnp.exp2(l2)
        t = 1.0 + e
        r = pl.reciprocal(t, approx=True)
        lb = labb[rows, :]
        lbw = jnp.concatenate([lb] * 5 + [lb[:, :64]], axis=1)
        col = (lax.broadcasted_iota(jnp.int32, (352, HALF), 1) + h * HALF).astype(F32)
        pos = lbw == col
        gh[h][rows, :] = (r * jnp.where(pos, -1.0, e)).astype(BF16)
        t3 = t.reshape(44, 8, HALF)
        p3 = jnp.where(pos, l2, 0.0).reshape(44, 8, HALF)
        total = -jnp.sum(p3, axis=0)
        for a in range(0, 44, 8):
            w = t3[a]
            for b in range(a + 1, min(a + 8, 44)):
                w = w * t3[b]
            total = total + jnp.log2(w)
        acc[...] += total

    def logits_span(first, count, h):
        @pl.loop(0, count)
        def _(i):
            logits(pl.multiple_of((first + i) * 352, 16), h)

    gwait(0)
    gstart(5)
    gwait(2)
    gstart(6)
    xcopy(0).wait_recv()
    gwait(4)
    gstart(7)
    gstart(8)
    gwait(1)
    gwait(3)
    for k in (1, 2, 3):
        start(xcopy(k))
    logits_span(PLACE[0], 1, 0)
    gwait(5)
    gstart(9)
    gwait(6)
    gstart(10)
    start(xcopy(4))
    for k in (1, 2, 3):
        xcopy(k).wait_recv()
    logits_span(PLACE[1], 3, 0)
    xcopy(4).wait_recv()
    logits_span(PLACE[4], 1, 0)
    gwait(7)
    start(xcopy(5))
    gwait(8)
    start(xcopy(6))
    xcopy(5).wait_recv()
    logits_span(PLACE[5], 1, 0)
    gwait(9)
    gwait(10)
    start(xcopy(7))
    xcopy(6).wait_recv()
    logits_span(PLACE[6], 1, 0)
    xcopy(7).wait_recv()
    logits_span(PLACE[7], 1, 0)
    logits_span(0, 8, 1)

    mine = jnp.broadcast_to(jnp.sum(acc[...]).reshape(1, 1), (8, 128))
    lossbuf[0] = mine
    y1 = 1 - 2 * (y % 2)
    x1 = 1 - 2 * (x % 2)
    pairs = (core, dev(dy=y1 + 4), dev(dy=4 - y1), dev(dx=x1 + 4), dev(dx=4 - x1), part[0], part[1])

    def pcopy(i):
        return copy(lossbuf.at[2 * i], lossbuf.at[2 * i + 1], ps.at[i], pr.at[i], pairs[i])

    def pnext(i):
        pcopy(i).wait_recv()
        lossbuf[2 * i + 2] = lossbuf[2 * i] + lossbuf[2 * i + 1]
        if i + 1 < 7:
            start(pcopy(i + 1))

    start(pcopy(0))

    rmoves = (
        (7, 7, 0, ROWS, part),
        (5, 5, 0, ROWS, minus),
        (6, 6, 0, ROWS, plus),
        (4, 4, 0, CUT, minus),
        (4, 4, CUT, ROWS - CUT, plus),
        (1, 1, 0, CUT, minus),
        (1, 1, CUT, ROWS - CUT, minus),
        (2, 2, 0, CUT, plus),
        (2, 2, CUT, ROWS - CUT, plus),
        (3, 3, 0, ROWS, part),
    )
    S7, S5, S6, S4A, S4B, S1A, S1B, S2A, S2B, S3 = range(10)

    def rcopy(f, i):
        k, _, lo, n, to = rmoves[i]
        sl = pl.ds(lo, n)
        return copy(stage.at[f, k - 1, sl, :], recv.at[f, k - 1, sl, :], rs.at[f, i], rr.at[f, i], to[f])

    def got(f, k, lo=0, n=ROWS):
        return recv[f, k - 1, lo : lo + n, :].astype(F32)

    def put(f, k, val, lo=0, n=ROWS):
        stage[f, k - 1, lo : lo + n, :] = val.astype(BF16)

    def ccopy(k):
        return copy(core_out.at[k], core_in.at[k], ccs.at[k], ccr.at[k], core)

    def du(row, n):
        rows = pl.ds(row, n)
        return nn(g0[rows, :], v[0:HALF, :]) + nn(g1[rows, :], v[HALF:, :])

    def du_step(k, nxt):
        if k is None:
            d = du(other_row(nxt), ROWS)
            core_out[nxt] = d.astype(BF16)
            start(ccopy(nxt))
            return None
        if nxt is None:
            d = du(same_row(k), ROWS)
        else:
            d = du(same_row(k), 352)
            core_out[nxt] = d[ROWS:].astype(BF16)
            start(ccopy(nxt))
        ccopy(k).wait_recv()
        return d[:ROWS] + core_in[k].astype(F32)

    def dv_half(h):
        @pl.loop(0, 4)
        def _(i):
            cols = pl.ds(pl.multiple_of(i * 256, 256), 256)
            dvf[:, cols] = tn(gh[h][...], u[:, cols])

        dvf[:, 1024:] = tn(gh[h][...], u[:, 1024:])

    def dvb(j):
        return dvf[j * ROWS : (j + 1) * ROWS, :]

    du_step(None, 7)
    pnext(0)
    put(0, 7, du_step(7, 5))
    start(rcopy(0, S7))
    pnext(1)
    put(0, 5, du_step(5, 6))
    start(rcopy(0, S5))
    pnext(2)
    put(0, 6, du_step(6, 4))
    start(rcopy(0, S6))
    pnext(3)

    dv_half(1)
    for k, i in ((7, S7), (5, S5), (6, S6)):
        put(1, k, dvb(k - 4))
        start(rcopy(1, i))
    pnext(4)

    rcopy(0, S7).wait_recv()
    put(0, 4, du_step(4, 1) + got(0, 7))
    start(rcopy(0, S4A))
    start(rcopy(0, S4B))
    pnext(5)
    rcopy(1, S7).wait_recv()
    put(1, 4, dvb(0) + got(1, 7))
    start(rcopy(1, S4A))
    start(rcopy(1, S4B))
    pnext(6)

    dv_half(0)

    d = du_step(1, 2)
    put(0, 1, d[CUT:], CUT, ROWS - CUT)
    start(rcopy(0, S1B))
    rcopy(0, S4A).wait_recv()
    put(0, 1, d[:CUT] + got(0, 4, 0, CUT), 0, CUT)
    start(rcopy(0, S1A))
    d = du_step(2, 3)
    put(0, 2, d[:CUT], 0, CUT)
    start(rcopy(0, S2A))
    rcopy(0, S4B).wait_recv()
    put(0, 2, d[CUT:] + got(0, 4, CUT, ROWS - CUT), CUT, ROWS - CUT)
    start(rcopy(0, S2B))

    rcopy(1, S4A).wait_recv()
    put(1, 1, dvb(1)[CUT:], CUT, ROWS - CUT)
    put(1, 1, dvb(1)[:CUT] + got(1, 4, 0, CUT), 0, CUT)
    start(rcopy(1, S1B))
    start(rcopy(1, S1A))
    rcopy(1, S4B).wait_recv()
    put(1, 2, dvb(2)[:CUT], 0, CUT)
    put(1, 2, dvb(2)[CUT:] + got(1, 4, CUT, ROWS - CUT), CUT, ROWS - CUT)
    start(rcopy(1, S2A))
    start(rcopy(1, S2B))
    rcopy(1, S5).wait_recv()
    rcopy(1, S6).wait_recv()
    put(1, 3, dvb(3) + got(1, 5) + got(1, 6))
    start(rcopy(1, S3))

    rcopy(0, S5).wait_recv()
    rcopy(0, S6).wait_recv()
    put(0, 3, du_step(3, 0) + got(0, 5) + got(0, 6))
    start(rcopy(0, S3))

    d = du_step(0, None)
    for i in (S1A, S1B, S2A, S2B, S3):
        rcopy(0, i).wait_recv()
    du_ref[...] = d + got(0, 1) + got(0, 2) + got(0, 3)
    for i in (S1A, S1B, S2A, S2B, S3):
        rcopy(1, i).wait_recv()
    dv_ref[...] = dvb(0) + got(1, 1) + got(1, 2) + got(1, 3)
    loss_ref[...] = lossbuf[14] * (LN2 / BATCH)

    for cp in sent:
        cp.wait_send()


def fused(log_scale, bias, images, texts, labels):
    vm = pl.BlockSpec(memory_space=pltpu.VMEM)
    sm = pl.BlockSpec(memory_space=pltpu.SMEM)
    dma = pltpu.SemaphoreType.DMA
    block = jax.ShapeDtypeStruct((ROWS, D), F32)
    return pl.pallas_call(
        kernel,
        out_shape=(block, block, jax.ShapeDtypeStruct((8, 128), F32)),
        in_specs=[sm, sm, vm, vm, vm],
        out_specs=(vm, vm, vm),
        scratch_shapes=[
            pltpu.VMEM((16 * ROWS, D), BF16),
            pltpu.VMEM((8 * ROWS, D), BF16),
            pltpu.VMEM((16 * ROWS, HALF), BF16),
            pltpu.VMEM((16 * ROWS, HALF), BF16),
            pltpu.VMEM((16, 8, 128), jnp.int32),
            pltpu.VMEM((16 * ROWS, 128), F32),
            pltpu.VMEM((8, HALF), F32),
            pltpu.VMEM((15, 8, 128), F32),
            pltpu.VMEM((HALF, D), F32),
            pltpu.VMEM((8, ROWS, D), BF16),
            pltpu.VMEM((8, ROWS, D), BF16),
            pltpu.VMEM((2, 7, ROWS, D), BF16),
            pltpu.VMEM((2, 7, ROWS, D), BF16),
            dma((2, 11)), dma((2, 11)),
            dma((8,)), dma((8,)),
            dma((15,)), dma((15,)),
            dma((2, 10)), dma((2, 10)),
            dma((8,)), dma((8,)),
            dma((7,)), dma((7,)),
        ],
        compiler_params=pltpu.CompilerParams(
            collective_id=0, has_side_effects=True, vmem_limit_bytes=60 << 20
        ),
        name="contrastive",
    )(log_scale, bias, images, texts, labels)


def back(rows, grad):
    rows = rows.astype(F32)
    inv = lax.rsqrt(jnp.sum(rows * rows, axis=-1, keepdims=True) + EPS)
    n = rows * inv
    return (grad - n * jnp.sum(n * grad, axis=-1, keepdims=True)) * inv


def body(images, texts, match, log_scale, bias):
    labels = jnp.pad(match, (0, 1024 - ROWS)).reshape(8, 128)
    du, dv, loss = fused(log_scale.reshape(1), bias.reshape(1), images, texts, labels)
    scale = jnp.exp(log_scale)
    return (loss[0, 0], back(images, scale * du), back(texts, scale * dv))


def solution(mesh):
    in_specs = (P(("img", "txt"), None), P(("txt", "img"), None), P(("img", "txt")), P(), P())
    out_specs = (P(), P(("img", "txt"), None), P(("txt", "img"), None))
    return jax.shard_map(body, mesh=mesh, in_specs=in_specs, out_specs=out_specs, check_vma=False)
```

```python
import functools

import jax
import jax.numpy as jnp
from jax import lax
from jax.experimental import pallas as pl
from jax.experimental.pallas import tpu as pltpu
from jax.sharding import PartitionSpec as P

EPS = 1e-06
ROWS = 176
D = 1152
HALF = 704
CUT = 96
LOG2E = 1.4426950408889634
LN2 = 0.6931471805599453
BATCH = 22528
MESH = pl.DeviceIdType.MESH
F32 = jnp.float32
BF16 = jnp.bfloat16

ORDER = (7, 5, 6, 4, 3, 1, 2, 0)
PLACE = {k: i for i, k in enumerate(ORDER)}


def other_row(k):
    return 352 * PLACE[k]


def same_row(k):
    return 352 * PLACE[k] + ROWS


def nt(a, b):
    return lax.dot_general(a, b, (((1,), (1,)), ((), ())), preferred_element_type=F32)


def nn(a, b):
    return lax.dot_general(a, b, (((1,), (0,)), ((), ())), preferred_element_type=F32)


def tn(a, b):
    return lax.dot_general(a, b, (((0,), (0,)), ((), ())), preferred_element_type=F32)


def kernel(
    ls_ref, bias_ref, img_ref, txt_ref, lab_ref,
    du_ref, dv_ref, loss_ref,
    u, v, g0, g1, labs, labb, acc, lossbuf,
    dvf, core_out, core_in, stage, recv,
    own, dvt, gs, gr, cs, cr, lsend, lrecv, rs, rr, ccs, ccr, ps, pr, ts, tr,
):
    im = lax.axis_index("img")
    tx = lax.axis_index("txt")
    x = im % 4
    z = (tx // 8) * 2 + im // 4
    y = (tx // 2) % 4
    c = tx % 2

    def dev(dx=0, dy=0, zz=None, dc=0):
        z2 = z if zz is None else zz
        return ((z2 % 2) * 4 + (x + dx) % 4, (z2 // 2) * 8 + ((y + dy) % 4) * 2 + (c + dc) % 2)

    zi = z + 1 - 2 * (z % 2)
    zt = 3 - z
    plus = (dev(dy=1), dev(dx=1))
    minus = (dev(dy=3), dev(dx=3))
    part = (dev(zz=zi), dev(zz=zt))
    core = dev(dc=1)

    group = []
    for dy, dz, k in ((1, 0, 1), (3, 0, 2), (0, 1, 3), (2, 0, 4), (1, 1, 5), (3, 1, 6), (2, 1, 7)):
        for dc in (0, 1):
            group.append((dev(dy=dy, zz=zi if dz else z, dc=dc), 2 * PLACE[k] + 1 - dc))
    group.append((core, 2 * PLACE[0]))

    labs[...] = jnp.zeros_like(labs)
    labs[2 * PLACE[0] + 1, 0:1, :] = lab_ref[0:1, 0:128]
    labs[2 * PLACE[0] + 1, 1:2, 0:48] = lab_ref[0:1, 128:ROWS]

    barrier = pltpu.get_barrier_semaphore()
    partners = [d for d, _ in group] + [plus[1], minus[1], part[1]]
    for d in partners:
        pl.semaphore_signal(barrier, inc=1, device_id=d, device_id_type=MESH)

    def norm(ref):
        rows = ref[...].astype(F32)
        return (rows * lax.rsqrt(jnp.sum(rows * rows, axis=-1, keepdims=True) + EPS)).astype(BF16)

    u[pl.ds(same_row(0), ROWS), :] = norm(img_ref)
    pl.semaphore_wait(barrier, len(partners))

    sent = []

    def copy(src, dst, ss, sr, d):
        return pltpu.make_async_remote_copy(
            src_ref=src, dst_ref=dst, send_sem=ss, recv_sem=sr, device_id=d, device_id_type=MESH
        )

    def start(cp):
        cp.start()
        sent.append(cp)

    def base(f, k):
        return same_row(k) if f == 0 else ROWS * k

    def piece(f, k, lo, n):
        return (u, v)[f].at[pl.ds(base(f, k) + lo, n), :]

    moves = (
        (0, 1, 0, CUT, plus),
        (0, 1, CUT, ROWS - CUT, plus),
        (0, 2, CUT, ROWS - CUT, minus),
        (0, 2, 0, CUT, minus),
        (0, 3, 0, ROWS, part),
        (1, 4, 0, CUT, plus),
        (2, 4, CUT, ROWS - CUT, minus),
        (3, 5, 0, ROWS, plus),
        (3, 6, 0, ROWS, minus),
        (4, 7, 0, CUT, part),
        (4, 7, CUT, ROWS - CUT, part),
    )

    def gcopy(f, i):
        a, b, lo, n, to = moves[i]
        return copy(piece(f, a, lo, n), piece(f, b, lo, n), gs.at[f, i], gr.at[f, i], to[f])

    def gstart(i):
        for f in (0, 1):
            start(gcopy(f, i))

    def gwait(i):
        for f in (0, 1):
            gcopy(f, i).wait_recv()

    def xcopy(k):
        return copy(
            u.at[pl.ds(same_row(k), ROWS), :], u.at[pl.ds(other_row(k), ROWS), :], cs.at[k], cr.at[k], core
        )

    for n, (d, slot) in enumerate(group):
        start(copy(labs.at[2 * PLACE[0] + 1], labs.at[slot], lsend.at[n], lrecv.at[n], d))
    for i in (0, 2, 4, 1, 3):
        start(gcopy(0, i))
    v[pl.ds(0, ROWS), :] = norm(txt_ref)
    for i in (0, 2, 4, 1, 3):
        start(gcopy(1, i))
    start(xcopy(0))

    scale = jnp.exp(jnp.full((8, 128), ls_ref[0], F32))
    c1 = scale[0:1, 0:1] * LOG2E
    c0 = jnp.full((1, 1), bias_ref[0] * LOG2E, F32)
    acc[...] = jnp.zeros_like(acc)

    gh = (g0, g1)
    one = jnp.minimum(im + 1, 1)

    def logits(row, h):
        rows = pl.ds(row, 352)
        s = nt(u[rows, :], v[h * HALF : (h + 1) * HALF, :])
        l2 = s * c1 + c0
        e = jnp.exp2(l2)
        t = 1.0 + e
        r = pl.reciprocal(t, approx=True)
        lb = labb[rows, :]
        lbw = jnp.concatenate([lb] * 5 + [lb[:, :64]], axis=1)
        col = (lax.broadcasted_iota(jnp.int32, (352, HALF), 1) + h * HALF).astype(F32)
        pos = lbw == col
        gh[h][rows, :] = (r * jnp.where(pos, -1.0, e)).astype(BF16)
        t3 = t.reshape(44, 8, HALF)
        p3 = jnp.where(pos, l2, 0.0).reshape(44, 8, HALF)
        total = -jnp.sum(p3, axis=0)
        for a in range(0, 44, 8):
            w = t3[a]
            for b in range(a + 1, min(a + 8, 44)):
                w = w * t3[b]
            total = total + jnp.log2(w)
        acc[...] += total

    def logits_span(first, count, h):
        @pl.loop(0, count * one)
        def _(i):
            logits(pl.multiple_of((first + i) * 352, 16), h)

    gwait(0)
    gstart(5)
    gwait(2)
    gstart(6)
    for n, (d, slot) in enumerate(group):
        copy(labs.at[2 * PLACE[0] + 1], labs.at[slot], lsend.at[n], lrecv.at[n], d).wait_recv()
    bases = []
    for dx, zz in ((0, z), (3, z), (1, z), (0, zt), (2, z), (3, zt), (1, zt), (2, zt)):
        i2, t2 = dev(dx=dx, zz=zz)
        bases.append((t2 * 8 + i2) * ROWS)
    for s in range(16):
        lab = labs[s]
        place = jnp.full((8, 128), -1, jnp.int32)
        for j, b in enumerate(bases):
            rel = lab - b
            place = jnp.where((rel >= 0) & (rel < ROWS), rel + ROWS * j, place)
        placef = place.astype(F32)
        first = jnp.broadcast_to(placef[0:1, :], (128, 128)).T
        second = jnp.broadcast_to(placef[1:2, :], (128, 128)).T
        labb[pl.ds(s * ROWS, 128), :] = first
        labb[pl.ds(s * ROWS + 128, 48), :] = second[0:48, :]

    gwait(4)
    gstart(7)
    gstart(8)
    gwait(1)
    gwait(3)
    for k in (1, 2, 3):
        start(xcopy(k))
    xcopy(0).wait_recv()
    logits_span(PLACE[0], 1, 0)
    for k in (1, 2, 3):
        xcopy(k).wait_recv()
    logits_span(PLACE[3], 1, 0)
    gwait(5)
    gstart(9)
    gwait(6)
    gstart(10)
    start(xcopy(4))
    logits_span(PLACE[1], 2, 0)
    xcopy(4).wait_recv()
    logits_span(PLACE[4], 1, 0)
    gwait(7)
    start(xcopy(5))
    gwait(8)
    start(xcopy(6))
    xcopy(5).wait_recv()
    logits_span(PLACE[5], 1, 0)
    gwait(9)
    gwait(10)
    start(xcopy(7))
    xcopy(6).wait_recv()
    logits_span(PLACE[6], 1, 0)
    xcopy(7).wait_recv()
    logits_span(PLACE[7], 1, 0)
    logits_span(0, 8, 1)

    mine = jnp.broadcast_to(jnp.sum(acc[...]).reshape(1, 1), (8, 128))
    lossbuf[0] = mine
    y1 = 1 - 2 * (y % 2)
    x1 = 1 - 2 * (x % 2)
    pairs = (core, dev(dy=y1 + 4), dev(dy=4 - y1), dev(dx=x1 + 4), dev(dx=4 - x1), part[0], part[1])

    def pcopy(i):
        return copy(lossbuf.at[2 * i], lossbuf.at[2 * i + 1], ps.at[i], pr.at[i], pairs[i])

    def pnext(i):
        pcopy(i).wait_recv()
        lossbuf[2 * i + 2] = lossbuf[2 * i] + lossbuf[2 * i + 1]
        if i + 1 < 7:
            start(pcopy(i + 1))

    start(pcopy(0))

    rmoves = (
        (7, 7, 0, ROWS, part),
        (5, 5, 0, ROWS, minus),
        (6, 6, 0, ROWS, plus),
        (4, 4, 0, CUT, minus),
        (4, 4, CUT, ROWS - CUT, plus),
        (1, 1, 0, CUT, minus),
        (1, 1, CUT, ROWS - CUT, minus),
        (2, 2, 0, CUT, plus),
        (2, 2, CUT, ROWS - CUT, plus),
        (3, 3, 0, ROWS, part),
    )
    S7, S5, S6, S4A, S4B, S1A, S1B, S2A, S2B, S3 = range(10)

    def rcopy(f, i):
        k, _, lo, n, to = rmoves[i]
        sl = pl.ds(lo, n)
        return copy(stage.at[f, k - 1, sl, :], recv.at[f, k - 1, sl, :], rs.at[f, i], rr.at[f, i], to[f])

    def got(f, k, lo=0, n=ROWS):
        return recv[f, k - 1, lo : lo + n, :].astype(F32)

    def put(f, k, val, lo=0, n=ROWS):
        stage[f, k - 1, lo : lo + n, :] = val.astype(BF16)

    def ccopy(k):
        return copy(core_out.at[k], core_in.at[k], ccs.at[k], ccr.at[k], core)

    def du_block(k, nxt):
        @pl.loop(0, one)
        def _(_i):
            first = other_row(nxt) if k is None else same_row(k)
            n = ROWS if k is None or nxt is None else 352
            rows = pl.ds(first, n)
            d = nn(g0[rows, :], v[0:HALF, :]) + nn(g1[rows, :], v[HALF:, :])
            if k is not None:
                own[k] = d[:ROWS]
            if nxt is not None:
                core_out[nxt] = d[n - ROWS :].astype(BF16)

        if nxt is not None:
            start(ccopy(nxt))

    def tcols(n):
        return slice(256 * n, min(256 * n + 256, D))

    tmoves = (
        (7, 0, ROWS, part),
        (5, 0, ROWS, minus),
        (6, 0, ROWS, plus),
        (3, 0, ROWS, part),
        (1, CUT, ROWS - CUT, minus),
        (2, 0, CUT, plus),
    )
    T7, T5, T6, T3, T1B, T2A = range(6)

    def tcopy(i, n):
        k, lo, rows, to = tmoves[i]
        sl, cols = pl.ds(lo, rows), pl.ds(256 * n, min(256, D - 256 * n))
        return copy(
            stage.at[1, k - 1, sl, cols], recv.at[1, k - 1, sl, cols], ts.at[i, n], tr.at[i, n], to[1]
        )

    def twait(i):
        for n in range(5):
            tcopy(i, n).wait_recv()

    def dv_late(n):
        cols = tcols(n)

        @pl.loop(0, one)
        def _(_i):
            d = tn(g1[...], u[:, cols])
            dvt[:, cols] = d[0:ROWS]
            for k in (5, 6, 7):
                stage[1, k - 1, :, cols] = d[(k - 4) * ROWS : (k - 3) * ROWS].astype(BF16)

        for i in (T7, T5, T6):
            start(tcopy(i, n))

    def dv_early(n):
        cols = tcols(n)
        for i in (T5, T6):
            tcopy(i, n).wait_recv()

        @pl.loop(0, one)
        def _(_i):
            d = tn(g0[...], u[:, cols])
            dvf[:, cols] = d[0 : 3 * ROWS]
            stage[1, 0, CUT:, cols] = d[ROWS + CUT : 2 * ROWS].astype(BF16)
            stage[1, 1, 0:CUT, cols] = d[2 * ROWS : 2 * ROWS + CUT].astype(BF16)
            both = recv[1, 4, :, cols].astype(F32) + recv[1, 5, :, cols].astype(F32)
            stage[1, 2, :, cols] = (d[3 * ROWS :] + both).astype(BF16)

        for i in (T3, T1B, T2A):
            start(tcopy(i, n))

    def mine_of(k, lo=0, n=ROWS):
        return own[k, lo : lo + n, :] + core_in[k, lo : lo + n, :].astype(F32)

    du_block(None, 7)
    dv_late(0)
    pnext(0)
    du_block(7, 5)
    ccopy(7).wait_recv()
    put(0, 7, mine_of(7))
    start(rcopy(0, S7))
    dv_late(1)
    pnext(1)
    du_block(5, 6)
    ccopy(5).wait_recv()
    put(0, 5, mine_of(5))
    start(rcopy(0, S5))
    dv_late(2)
    pnext(2)
    du_block(6, 4)
    ccopy(6).wait_recv()
    put(0, 6, mine_of(6))
    start(rcopy(0, S6))
    dv_late(3)
    pnext(3)
    dv_late(4)
    pnext(4)
    du_block(4, 3)
    du_block(3, 1)
    pnext(5)

    ccopy(4).wait_recv()
    rcopy(0, S7).wait_recv()
    put(0, 4, mine_of(4) + got(0, 7))
    start(rcopy(0, S4A))
    start(rcopy(0, S4B))
    twait(T7)
    put(1, 4, dvt[...] + got(1, 7))
    start(rcopy(1, S4A))
    start(rcopy(1, S4B))
    pnext(6)

    dv_early(0)
    du_block(1, 2)
    ccopy(1).wait_recv()
    put(0, 1, mine_of(1, CUT, ROWS - CUT), CUT, ROWS - CUT)
    start(rcopy(0, S1B))
    dv_early(1)
    ccopy(3).wait_recv()
    rcopy(0, S5).wait_recv()
    rcopy(0, S6).wait_recv()
    put(0, 3, mine_of(3) + got(0, 5) + got(0, 6))
    start(rcopy(0, S3))
    du_block(2, 0)
    ccopy(2).wait_recv()
    put(0, 2, mine_of(2, 0, CUT), 0, CUT)
    start(rcopy(0, S2A))
    dv_early(2)
    dv_early(3)

    rcopy(0, S4A).wait_recv()
    put(0, 1, mine_of(1, 0, CUT) + got(0, 4, 0, CUT), 0, CUT)
    start(rcopy(0, S1A))
    rcopy(0, S4B).wait_recv()
    put(0, 2, mine_of(2, CUT, ROWS - CUT) + got(0, 4, CUT, ROWS - CUT), CUT, ROWS - CUT)
    start(rcopy(0, S2B))
    dv_early(4)
    rcopy(1, S4A).wait_recv()
    put(1, 1, dvf[ROWS : ROWS + CUT, :] + got(1, 4, 0, CUT), 0, CUT)
    start(rcopy(1, S1A))
    rcopy(1, S4B).wait_recv()
    put(1, 2, dvf[2 * ROWS + CUT : 3 * ROWS, :] + got(1, 4, CUT, ROWS - CUT), CUT, ROWS - CUT)
    start(rcopy(1, S2B))
    du_block(0, None)

    ccopy(0).wait_recv()
    loss_ref[0] = jnp.max(lossbuf[14]) * (LN2 / BATCH)

    def finish(f, ref, out, grad):
        rows = ref[...].astype(F32)
        inv = lax.rsqrt(jnp.sum(rows * rows, axis=-1, keepdims=True) + EPS)
        n = rows * inv
        if f == 0:
            for i in (S1A, S1B, S2A, S2B, S3):
                rcopy(0, i).wait_recv()
        else:
            for i in (S1A, S2B):
                rcopy(1, i).wait_recv()
            for i in (T3, T1B, T2A):
                twait(i)
        grad = (grad + got(f, 1) + got(f, 2) + got(f, 3)) * scale[0:1, 0:1]
        out[...] = (grad - n * jnp.sum(n * grad, axis=-1, keepdims=True)) * inv

    finish(0, img_ref, du_ref, mine_of(0))
    finish(1, txt_ref, dv_ref, dvf[0:ROWS, :])

    for cp in sent:
        cp.wait_send()


def fused(log_scale, bias, images, texts, labels):
    vm = pl.BlockSpec(memory_space=pltpu.VMEM)
    sm = pl.BlockSpec(memory_space=pltpu.SMEM)
    dma = pltpu.SemaphoreType.DMA
    block = jax.ShapeDtypeStruct((ROWS, D), F32)
    return pl.pallas_call(
        kernel,
        out_shape=(block, block, jax.ShapeDtypeStruct((1,), F32)),
        in_specs=[sm, sm, vm, vm, vm],
        out_specs=(vm, vm, sm),
        scratch_shapes=[
            pltpu.VMEM((16 * ROWS, D), BF16),
            pltpu.VMEM((8 * ROWS, D), BF16),
            pltpu.VMEM((16 * ROWS, HALF), BF16),
            pltpu.VMEM((16 * ROWS, HALF), BF16),
            pltpu.VMEM((16, 8, 128), jnp.int32),
            pltpu.VMEM((16 * ROWS, 128), F32),
            pltpu.VMEM((8, HALF), F32),
            pltpu.VMEM((15, 8, 128), F32),
            pltpu.VMEM((3 * ROWS, D), F32),
            pltpu.VMEM((8, ROWS, D), BF16),
            pltpu.VMEM((8, ROWS, D), BF16),
            pltpu.VMEM((2, 7, ROWS, D), BF16),
            pltpu.VMEM((2, 7, ROWS, D), BF16),
            pltpu.VMEM((8, ROWS, D), F32),
            pltpu.VMEM((ROWS, D), F32),
            dma((2, 11)), dma((2, 11)),
            dma((8,)), dma((8,)),
            dma((15,)), dma((15,)),
            dma((2, 10)), dma((2, 10)),
            dma((8,)), dma((8,)),
            dma((7,)), dma((7,)),
            dma((6, 5)), dma((6, 5)),
        ],
        compiler_params=pltpu.CompilerParams(
            collective_id=0, has_side_effects=True, vmem_limit_bytes=60 << 20
        ),
        name="contrastive",
    )(log_scale, bias, images, texts, labels)


def body(images, texts, match, log_scale, bias):
    du, dv, loss = fused(log_scale.reshape(1), bias.reshape(1), images, texts, match.reshape(1, ROWS))
    return (loss.reshape(()), du, dv)


def solution(mesh):
    in_specs = (P(("img", "txt"), None), P(("txt", "img"), None), P(("img", "txt")), P(), P())
    out_specs = (P(), P(("img", "txt"), None), P(("txt", "img"), None))
    return jax.shard_map(body, mesh=mesh, in_specs=in_specs, out_specs=out_specs, check_vma=False)
```

```python
import functools

import jax
import jax.numpy as jnp
from jax import lax
from jax.experimental import pallas as pl
from jax.experimental.pallas import tpu as pltpu
from jax.sharding import PartitionSpec as P

EPS = 1e-06
ROWS = 176
D = 1152
HALF = 704
CUT = 96
LOG2E = 1.4426950408889634
LN2 = 0.6931471805599453
BATCH = 22528
MESH = pl.DeviceIdType.MESH
F32 = jnp.float32
BF16 = jnp.bfloat16

ORDER = (7, 5, 6, 4, 3, 1, 2, 0)
PLACE = {k: i for i, k in enumerate(ORDER)}


def other_row(k):
    return 352 * PLACE[k]


def same_row(k):
    return 352 * PLACE[k] + ROWS


EARLY = other_row(4)


def nt(a, b):
    return lax.dot_general(a, b, (((1,), (1,)), ((), ())), preferred_element_type=F32)


def nn(a, b):
    return lax.dot_general(a, b, (((1,), (0,)), ((), ())), preferred_element_type=F32)


def tn(a, b):
    return lax.dot_general(a, b, (((0,), (0,)), ((), ())), preferred_element_type=F32)


def kernel(
    ls_ref, bias_ref, img_ref, txt_ref, lab_ref,
    du_ref, dv_ref, loss_ref,
    u, v, g0, g1, labs, labb, acc, lossbuf,
    dvf, core_out, core_in, stage, recv,
    own, pdu, dvt, gs, gr, cs, cr, lsend, lrecv, rs, rr, ccs, ccr, ps, pr, ts, tr,
):
    im = lax.axis_index("img")
    tx = lax.axis_index("txt")
    x = im % 4
    z = (tx // 8) * 2 + im // 4
    y = (tx // 2) % 4
    c = tx % 2

    def dev(dx=0, dy=0, zz=None, dc=0):
        z2 = z if zz is None else zz
        return ((z2 % 2) * 4 + (x + dx) % 4, (z2 // 2) * 8 + ((y + dy) % 4) * 2 + (c + dc) % 2)

    zi = z + 1 - 2 * (z % 2)
    zt = 3 - z
    plus = (dev(dy=1), dev(dx=1))
    minus = (dev(dy=3), dev(dx=3))
    part = (dev(zz=zi), dev(zz=zt))
    core = dev(dc=1)

    group = []
    for dy, dz, k in ((1, 0, 1), (3, 0, 2), (0, 1, 3), (2, 0, 4), (1, 1, 5), (3, 1, 6), (2, 1, 7)):
        for dc in (0, 1):
            group.append((dev(dy=dy, zz=zi if dz else z, dc=dc), 2 * PLACE[k] + 1 - dc))
    group.append((core, 2 * PLACE[0]))

    labs[...] = jnp.zeros_like(labs)
    labs[2 * PLACE[0] + 1, 0:1, :] = lab_ref[0:1, 0:128]
    labs[2 * PLACE[0] + 1, 1:2, 0:48] = lab_ref[0:1, 128:ROWS]

    barrier = pltpu.get_barrier_semaphore()
    partners = [d for d, _ in group] + [plus[1], minus[1], part[1]]
    for d in partners:
        pl.semaphore_signal(barrier, inc=1, device_id=d, device_id_type=MESH)

    def norm(ref):
        rows = ref[...].astype(F32)
        return (rows * lax.rsqrt(jnp.sum(rows * rows, axis=-1, keepdims=True) + EPS)).astype(BF16)

    u[pl.ds(same_row(0), ROWS), :] = norm(img_ref)
    pl.semaphore_wait(barrier, len(partners))

    sent = []

    def copy(src, dst, ss, sr, d):
        return pltpu.make_async_remote_copy(
            src_ref=src, dst_ref=dst, send_sem=ss, recv_sem=sr, device_id=d, device_id_type=MESH
        )

    def start(cp):
        cp.start()
        sent.append(cp)

    def base(f, k):
        return same_row(k) if f == 0 else ROWS * k

    def piece(f, k, lo, n):
        return (u, v)[f].at[pl.ds(base(f, k) + lo, n), :]

    moves = (
        (0, 1, 0, CUT, plus),
        (0, 1, CUT, ROWS - CUT, plus),
        (0, 2, CUT, ROWS - CUT, minus),
        (0, 2, 0, CUT, minus),
        (0, 3, 0, ROWS, part),
        (1, 4, 0, 48, plus),
        (2, 4, 96, 48, minus),
        (3, 5, 0, ROWS, plus),
        (3, 6, 0, ROWS, minus),
        (1, 4, 48, 48, plus),
        (2, 4, 144, 32, minus),
        (4, 7, 0, 48, part),
        (4, 7, 96, 48, part),
        (4, 7, 48, 48, part),
        (4, 7, 144, 32, part),
    )

    def gcopy(f, i):
        a, b, lo, n, to = moves[i]
        return copy(piece(f, a, lo, n), piece(f, b, lo, n), gs.at[f, i], gr.at[f, i], to[f])

    def gstart(i):
        for f in (0, 1):
            start(gcopy(f, i))

    def gwait(i):
        for f in (0, 1):
            gcopy(f, i).wait_recv()

    def xcopy(k):
        return copy(
            u.at[pl.ds(same_row(k), ROWS), :], u.at[pl.ds(other_row(k), ROWS), :], cs.at[k], cr.at[k], core
        )

    for n, (d, slot) in enumerate(group):
        start(copy(labs.at[2 * PLACE[0] + 1], labs.at[slot], lsend.at[n], lrecv.at[n], d))
    for i in (0, 2, 4, 1, 3):
        start(gcopy(0, i))
    v[pl.ds(0, ROWS), :] = norm(txt_ref)
    for i in (0, 2, 4, 1, 3):
        start(gcopy(1, i))
    start(xcopy(0))

    scale = jnp.exp(jnp.full((8, 128), ls_ref[0], F32))
    c1 = scale[0:1, 0:1] * LOG2E
    c0 = jnp.full((1, 1), bias_ref[0] * LOG2E, F32)
    acc[...] = jnp.zeros_like(acc)

    gh = (g0, g1)
    one = jnp.minimum(im + 1, 1)

    def logits(row, h):
        rows = pl.ds(row, 352)
        s = nt(u[rows, :], v[h * HALF : (h + 1) * HALF, :])
        l2 = s * c1 + c0
        e = jnp.exp2(l2)
        t = 1.0 + e
        r = pl.reciprocal(t, approx=True)
        lb = labb[rows, :]
        lbw = jnp.concatenate([lb] * 5 + [lb[:, :64]], axis=1)
        col = (lax.broadcasted_iota(jnp.int32, (352, HALF), 1) + h * HALF).astype(F32)
        pos = lbw == col
        gh[h][rows, :] = (r * jnp.where(pos, -1.0, e)).astype(BF16)
        t3 = t.reshape(44, 8, HALF)
        p3 = jnp.where(pos, l2, 0.0).reshape(44, 8, HALF)
        total = -jnp.sum(p3, axis=0)
        for a in range(0, 44, 8):
            w = t3[a]
            for b in range(a + 1, min(a + 8, 44)):
                w = w * t3[b]
            total = total + jnp.log2(w)
        acc[...] += total

    def logits_span(first, count, h):
        @pl.loop(0, count * one)
        def _(i):
            logits(pl.multiple_of((first + i) * 352, 16), h)

    gwait(0)
    gstart(5)
    gstart(9)
    gwait(2)
    gstart(6)
    gstart(10)
    for n, (d, slot) in enumerate(group):
        copy(labs.at[2 * PLACE[0] + 1], labs.at[slot], lsend.at[n], lrecv.at[n], d).wait_recv()
    bases = []
    for dx, zz in ((0, z), (3, z), (1, z), (0, zt), (2, z), (3, zt), (1, zt), (2, zt)):
        i2, t2 = dev(dx=dx, zz=zz)
        bases.append((t2 * 8 + i2) * ROWS)
    for s in range(16):
        lab = labs[s]
        place = jnp.full((8, 128), -1, jnp.int32)
        for j, b in enumerate(bases):
            rel = lab - b
            place = jnp.where((rel >= 0) & (rel < ROWS), rel + ROWS * j, place)
        placef = place.astype(F32)
        first = jnp.broadcast_to(placef[0:1, :], (128, 128)).T
        second = jnp.broadcast_to(placef[1:2, :], (128, 128)).T
        labb[pl.ds(s * ROWS, 128), :] = first
        labb[pl.ds(s * ROWS + 128, 48), :] = second[0:48, :]

    gwait(4)
    gstart(7)
    gstart(8)
    gwait(1)
    gwait(3)
    for k in (1, 2, 3):
        start(xcopy(k))
    xcopy(0).wait_recv()
    logits_span(PLACE[0], 1, 0)
    gwait(5)
    gstart(11)
    gwait(6)
    gstart(12)
    for k in (1, 2, 3):
        xcopy(k).wait_recv()
    logits_span(PLACE[3], 2, 0)
    gwait(9)
    gstart(13)
    gwait(10)
    gstart(14)
    start(xcopy(4))
    logits_span(PLACE[2], 1, 0)
    xcopy(4).wait_recv()
    logits_span(PLACE[4], 1, 0)

    @pl.loop(0, 4 * one)
    def _(i):
        at = pl.multiple_of(i * 352, 16)
        pdu[pl.ds(at, 352), :] = nn(g0[pl.ds(same_row(4) + at, 352), :], v[0:HALF, :])

    @pl.loop(0, one)
    def _(_i):
        pdu[8 * ROWS :, :] = nn(g0[same_row(0) :, :], v[0:HALF, :])

    gwait(7)
    start(xcopy(5))
    gwait(8)
    start(xcopy(6))
    xcopy(5).wait_recv()
    logits_span(PLACE[5], 1, 0)
    for i in (11, 12, 13, 14):
        gwait(i)
    start(xcopy(7))
    logits_span(PLACE[4], 5, 1)
    xcopy(6).wait_recv()
    logits_span(PLACE[6], 1, 0)
    xcopy(7).wait_recv()
    logits_span(PLACE[7], 1, 0)
    logits_span(0, 3, 1)

    mine = jnp.broadcast_to(jnp.sum(acc[...]).reshape(1, 1), (8, 128))
    lossbuf[0] = mine
    y1 = 1 - 2 * (y % 2)
    x1 = 1 - 2 * (x % 2)
    pairs = (core, dev(dy=y1 + 4), dev(dy=4 - y1), dev(dx=x1 + 4), dev(dx=4 - x1), part[0], part[1])

    def pcopy(i):
        return copy(lossbuf.at[2 * i], lossbuf.at[2 * i + 1], ps.at[i], pr.at[i], pairs[i])

    def pnext(i):
        pcopy(i).wait_recv()
        lossbuf[2 * i + 2] = lossbuf[2 * i] + lossbuf[2 * i + 1]
        if i + 1 < 7:
            start(pcopy(i + 1))

    start(pcopy(0))

    rmoves = (
        (7, 7, 0, CUT, part),
        (7, 7, CUT, ROWS - CUT, part),
        (5, 5, 0, ROWS, minus),
        (6, 6, 0, ROWS, plus),
        (4, 4, 0, CUT, minus),
        (4, 4, CUT, ROWS - CUT, plus),
        (1, 1, 0, CUT, minus),
        (1, 1, CUT, ROWS - CUT, minus),
        (2, 2, 0, CUT, plus),
        (2, 2, CUT, ROWS - CUT, plus),
        (3, 3, 0, ROWS, part),
    )
    S7A, S7B, S5, S6, S4A, S4B, S1A, S1B, S2A, S2B, S3 = range(11)

    def rcopy(f, i):
        k, _, lo, n, to = rmoves[i]
        sl = pl.ds(lo, n)
        return copy(stage.at[f, k - 1, sl, :], recv.at[f, k - 1, sl, :], rs.at[f, i], rr.at[f, i], to[f])

    def got(f, k, lo=0, n=ROWS):
        return recv[f, k - 1, lo : lo + n, :].astype(F32)

    def put(f, k, val, lo=0, n=ROWS):
        stage[f, k - 1, lo : lo + n, :] = val.astype(BF16)

    def ccopy(k):
        return copy(core_out.at[k], core_in.at[k], ccs.at[k], ccr.at[k], core)

    def du_block(k, nxt):
        @pl.loop(0, one)
        def _(_i):
            first = other_row(nxt) if k is None else same_row(k)
            n = ROWS if k is None or nxt is None else 352
            rows = pl.ds(first, n)
            d = nn(g1[rows, :], v[HALF:, :])
            if k in (None, 5, 6, 7):
                d = d + nn(g0[rows, :], v[0:HALF, :])
                if k is not None:
                    own[k - 5] = d[:ROWS]
            else:
                at = first - same_row(4)
                d = d + pdu[at : at + n, :]
                pdu[at : at + ROWS, :] = d[:ROWS]
            if nxt is not None:
                core_out[nxt] = d[n - ROWS :].astype(BF16)

        if nxt is not None:
            start(ccopy(nxt))

    def tcols(n):
        return slice(256 * n, min(256 * n + 256, D))

    tmoves = (
        (7, 0, ROWS, part),
        (5, 0, ROWS, minus),
        (6, 0, ROWS, plus),
        (3, 0, ROWS, part),
        (1, CUT, ROWS - CUT, minus),
        (2, 0, CUT, plus),
        (4, 0, CUT, minus),
        (4, CUT, ROWS - CUT, plus),
    )
    T7, T5, T6, T3, T1B, T2A, T4A, T4B = range(8)

    def tcopy(i, n):
        k, lo, rows, to = tmoves[i]
        sl, cols = pl.ds(lo, rows), pl.ds(256 * n, min(256, D - 256 * n))
        return copy(
            stage.at[1, k - 1, sl, cols], recv.at[1, k - 1, sl, cols], ts.at[i, n], tr.at[i, n], to[1]
        )

    def twait(i):
        for n in range(5):
            tcopy(i, n).wait_recv()

    def dv_late(n, step=None):
        cols = tcols(n)

        @pl.loop(0, one)
        def _(_i):
            d = tn(g1[...], u[:, cols])
            dvt[:, cols] = d[0:ROWS]
            for k in (5, 6, 7):
                stage[1, k - 1, :, cols] = d[(k - 4) * ROWS : (k - 3) * ROWS].astype(BF16)

        if step is not None:
            pnext(step)
        for i in (T7, T5, T6):
            start(tcopy(i, n))

    def dv_early(n):
        cols = tcols(n)
        for i in (T5, T6):
            tcopy(i, n).wait_recv()

        @pl.loop(0, one)
        def _(_i):
            d = tn(g0[...], u[:, cols])
            dvf[0 : 3 * ROWS, cols] = d[0 : 3 * ROWS]
            stage[1, 0, CUT:, cols] = d[ROWS + CUT : 2 * ROWS].astype(BF16)
            stage[1, 1, 0:CUT, cols] = d[2 * ROWS : 2 * ROWS + CUT].astype(BF16)
            both = recv[1, 4, :, cols].astype(F32) + recv[1, 5, :, cols].astype(F32)
            stage[1, 2, :, cols] = (d[3 * ROWS :] + both).astype(BF16)

        for i in (T3, T1B, T2A):
            start(tcopy(i, n))

    def mine_of(k, lo=0, n=ROWS):
        if k >= 5:
            mine = own[k - 5, lo : lo + n, :]
        else:
            at = same_row(k) - same_row(4) + lo
            mine = pdu[at : at + n, :]
        return mine + core_in[k, lo : lo + n, :].astype(F32)

    du_block(None, 7)
    dv_late(0, 0)
    du_block(7, 5)
    ccopy(7).wait_recv()
    put(0, 7, mine_of(7))
    start(rcopy(0, S7A))
    start(rcopy(0, S7B))
    du_block(5, 6)
    ccopy(5).wait_recv()
    put(0, 5, mine_of(5))
    pnext(1)
    start(rcopy(0, S5))
    du_block(6, 4)
    ccopy(6).wait_recv()
    put(0, 6, mine_of(6))
    start(rcopy(0, S6))
    dv_late(1, 2)
    dv_late(2)
    dv_late(3)
    dv_late(4, 3)
    du_block(4, 3)

    ccopy(4).wait_recv()
    rcopy(0, S7A).wait_recv()
    put(0, 4, mine_of(4, 0, CUT) + got(0, 7, 0, CUT), 0, CUT)
    start(rcopy(0, S4A))
    du_block(3, 1)
    rcopy(0, S7B).wait_recv()
    put(0, 4, mine_of(4, CUT, ROWS - CUT) + got(0, 7, CUT, ROWS - CUT), CUT, ROWS - CUT)
    start(rcopy(0, S4B))

    def text_four(n):
        cols = tcols(n)
        tcopy(T7, n).wait_recv()
        stage[1, 3, :, cols] = (dvt[:, cols] + recv[1, 6, :, cols].astype(F32)).astype(BF16)
        start(tcopy(T4A, n))
        start(tcopy(T4B, n))

    text_four(0)
    text_four(1)
    dv_early(0)
    text_four(2)
    du_block(1, 2)
    ccopy(1).wait_recv()
    put(0, 1, mine_of(1, CUT, ROWS - CUT), CUT, ROWS - CUT)
    start(rcopy(0, S1B))
    text_four(3)
    dv_early(1)
    text_four(4)
    ccopy(3).wait_recv()
    rcopy(0, S5).wait_recv()
    rcopy(0, S6).wait_recv()
    put(0, 3, mine_of(3) + got(0, 5) + got(0, 6))
    pnext(4)
    start(rcopy(0, S3))
    dv_early(2)
    du_block(2, 0)
    ccopy(2).wait_recv()
    put(0, 2, mine_of(2, 0, CUT), 0, CUT)
    start(rcopy(0, S2A))
    dv_early(3)

    rcopy(0, S4A).wait_recv()
    put(0, 1, mine_of(1, 0, CUT) + got(0, 4, 0, CUT), 0, CUT)
    start(rcopy(0, S1A))
    rcopy(0, S4B).wait_recv()
    put(0, 2, mine_of(2, CUT, ROWS - CUT) + got(0, 4, CUT, ROWS - CUT), CUT, ROWS - CUT)
    start(rcopy(0, S2B))
    dv_early(4)
    pnext(5)
    du_block(0, None)
    twait(T4A)
    put(1, 1, dvf[ROWS : ROWS + CUT, :] + got(1, 4, 0, CUT), 0, CUT)
    start(rcopy(1, S1A))
    twait(T4B)
    put(1, 2, dvf[2 * ROWS + CUT : 3 * ROWS, :] + got(1, 4, CUT, ROWS - CUT), CUT, ROWS - CUT)
    start(rcopy(1, S2B))

    ccopy(0).wait_recv()

    def finish(f, ref, out, grad, lo, n):
        rows = ref[lo : lo + n, :].astype(F32)
        inv = lax.rsqrt(jnp.sum(rows * rows, axis=-1, keepdims=True) + EPS)
        unit = rows * inv
        grad = (grad + got(f, 1, lo, n) + got(f, 2, lo, n) + got(f, 3, lo, n)) * scale[0:1, 0:1]
        out[lo : lo + n, :] = (grad - unit * jnp.sum(unit * grad, axis=-1, keepdims=True)) * inv

    rest = ROWS - CUT
    for i in (S1B, S2A, S3, S1A):
        rcopy(0, i).wait_recv()
    finish(0, img_ref, du_ref, mine_of(0, 0, CUT), 0, CUT)
    for i in (T3, T1B, T2A):
        twait(i)
    rcopy(1, S1A).wait_recv()
    finish(1, txt_ref, dv_ref, dvf[0:CUT, :], 0, CUT)
    rcopy(0, S2B).wait_recv()
    finish(0, img_ref, du_ref, mine_of(0, CUT, rest), CUT, rest)
    rcopy(1, S2B).wait_recv()
    finish(1, txt_ref, dv_ref, dvf[CUT:ROWS, :], CUT, rest)
    pnext(6)
    loss_ref[0] = jnp.max(lossbuf[14]) * (LN2 / BATCH)

    for cp in sent:
        cp.wait_send()


def fused(log_scale, bias, images, texts, labels):
    vm = pl.BlockSpec(memory_space=pltpu.VMEM)
    sm = pl.BlockSpec(memory_space=pltpu.SMEM)
    dma = pltpu.SemaphoreType.DMA
    block = pltpu.VMEM((ROWS, D), F32)
    return pl.pallas_call(
        kernel,
        out_shape=(block, block, jax.ShapeDtypeStruct((1,), F32)),
        in_specs=[sm, sm, vm, vm, vm],
        out_specs=(vm, vm, sm),
        scratch_shapes=[
            pltpu.VMEM((16 * ROWS, D), BF16),
            pltpu.VMEM((8 * ROWS, D), BF16),
            pltpu.VMEM((16 * ROWS, HALF), BF16),
            pltpu.VMEM((16 * ROWS, HALF), BF16),
            pltpu.VMEM((16, 8, 128), jnp.int32),
            pltpu.VMEM((16 * ROWS, 128), F32),
            pltpu.VMEM((8, HALF), F32),
            pltpu.VMEM((15, 8, 128), F32),
            pltpu.VMEM((HALF, D), F32),
            pltpu.VMEM((8, ROWS, D), BF16),
            pltpu.VMEM((8, ROWS, D), BF16),
            pltpu.VMEM((2, 7, ROWS, D), BF16),
            pltpu.VMEM((2, 7, ROWS, D), BF16),
            pltpu.VMEM((3, ROWS, D), F32),
            pltpu.VMEM((9 * ROWS, D), F32),
            pltpu.VMEM((ROWS, D), F32),
            dma((2, 15)), dma((2, 15)),
            dma((8,)), dma((8,)),
            dma((15,)), dma((15,)),
            dma((2, 11)), dma((2, 11)),
            dma((8,)), dma((8,)),
            dma((7,)), dma((7,)),
            dma((8, 5)), dma((8, 5)),
        ],
        compiler_params=pltpu.CompilerParams(
            collective_id=0, has_side_effects=True, vmem_limit_bytes=60 << 20
        ),
        name="contrastive",
    )(log_scale, bias, images, texts, labels)


def body(images, texts, match, log_scale, bias):
    du, dv, loss = fused(log_scale.reshape(1), bias.reshape(1), images, texts, match.reshape(1, ROWS))
    return (loss.reshape(()), du, dv)


def solution(mesh):
    in_specs = (P(("img", "txt"), None), P(("txt", "img"), None), P(("img", "txt")), P(), P())
    out_specs = (P(), P(("img", "txt"), None), P(("txt", "img"), None))
    return jax.shard_map(body, mesh=mesh, in_specs=in_specs, out_specs=out_specs, check_vma=False)
```

```python
import functools

import jax
import jax.numpy as jnp
from jax import lax
from jax.experimental import pallas as pl
from jax.experimental.pallas import tpu as pltpu
from jax.sharding import PartitionSpec as P

EPS = 1e-06
ROWS = 176
D = 1152
HALF = 704
CUT = 96
CUTI = 112
SIDE = 32
LOG2E = 1.4426950408889634
LN2 = 0.6931471805599453
BATCH = 22528
MESH = pl.DeviceIdType.MESH
F32 = jnp.float32
BF16 = jnp.bfloat16

ORDER = (7, 5, 6, 4, 3, 1, 2, 0)
PLACE = {k: i for i, k in enumerate(ORDER)}


def other_row(k):
    return 352 * PLACE[k]


def same_row(k):
    return 352 * PLACE[k] + ROWS


EARLY = other_row(4)


def nt(a, b):
    return lax.dot_general(a, b, (((1,), (1,)), ((), ())), preferred_element_type=F32)


def nn(a, b):
    return lax.dot_general(a, b, (((1,), (0,)), ((), ())), preferred_element_type=F32)


def tn(a, b):
    return lax.dot_general(a, b, (((0,), (0,)), ((), ())), preferred_element_type=F32)


def kernel(
    ls_ref, bias_ref, img_ref, txt_ref, lab_ref,
    du_ref, dv_ref, loss_ref,
    u, v, g0, g1, labs, labb, acc, lossbuf,
    dvf, core_out, core_in, stage, recv,
    own, pdu, dvt, gs, gr, cs, cr, lsend, lrecv, rs, rr, ccs, ccr, ps, pr, ts, tr,
):
    im = lax.axis_index("img")
    tx = lax.axis_index("txt")
    x = im % 4
    z = (tx // 8) * 2 + im // 4
    y = (tx // 2) % 4
    c = tx % 2

    def dev(dx=0, dy=0, zz=None, dc=0):
        z2 = z if zz is None else zz
        return ((z2 % 2) * 4 + (x + dx) % 4, (z2 // 2) * 8 + ((y + dy) % 4) * 2 + (c + dc) % 2)

    zi = z + 1 - 2 * (z % 2)
    zt = 3 - z
    plus = (dev(dy=1), dev(dx=1))
    minus = (dev(dy=3), dev(dx=3))
    part = (dev(zz=zi), dev(zz=zt))
    core = dev(dc=1)

    group = []
    for dy, dz, k in ((1, 0, 1), (3, 0, 2), (0, 1, 3), (2, 0, 4), (1, 1, 5), (3, 1, 6), (2, 1, 7)):
        for dc in (0, 1):
            group.append((dev(dy=dy, zz=zi if dz else z, dc=dc), 2 * PLACE[k] + 1 - dc))
    group.append((core, 2 * PLACE[0]))

    labs[...] = jnp.zeros_like(labs)
    labs[2 * PLACE[0] + 1, 0:1, :] = lab_ref[0:1, 0:128]
    labs[2 * PLACE[0] + 1, 1:2, 0:48] = lab_ref[0:1, 128:ROWS]

    barrier = pltpu.get_barrier_semaphore()
    partners = [d for d, _ in group] + [plus[1], minus[1], part[1]]
    for d in partners:
        pl.semaphore_signal(barrier, inc=1, device_id=d, device_id_type=MESH)

    def norm(ref):
        rows = ref[...].astype(F32)
        return (rows * lax.rsqrt(jnp.sum(rows * rows, axis=-1, keepdims=True) + EPS)).astype(BF16)

    u[pl.ds(same_row(0), ROWS), :] = norm(img_ref)
    pl.semaphore_wait(barrier, len(partners))

    sent = []

    def copy(src, dst, ss, sr, d):
        return pltpu.make_async_remote_copy(
            src_ref=src, dst_ref=dst, send_sem=ss, recv_sem=sr, device_id=d, device_id_type=MESH
        )

    def start(cp):
        cp.start()
        sent.append(cp)

    def base(f, k):
        return same_row(k) if f == 0 else ROWS * k

    def piece(f, k, lo, n):
        return (u, v)[f].at[pl.ds(base(f, k) + lo, n), :]

    moves = (
        (0, 1, 0, CUT, plus),
        (0, 1, CUT, ROWS - CUT, plus),
        (0, 2, CUT, ROWS - CUT, minus),
        (0, 2, 0, CUT, minus),
        (0, 3, 0, ROWS, part),
        (1, 4, 0, 48, plus),
        (2, 4, 96, 48, minus),
        (3, 5, SIDE, ROWS - SIDE, plus),
        (3, 6, 0, ROWS - SIDE, minus),
        (1, 4, 48, 48, plus),
        (2, 4, 144, 32, minus),
        (4, 7, 0, 48, part),
        (4, 7, 96, 48, part),
        (4, 7, 48, 48, part),
        (4, 7, 144, 32, part),
        (1, 5, 0, SIDE, part),
        (2, 6, ROWS - SIDE, SIDE, part),
    )

    def gcopy(f, i):
        a, b, lo, n, to = moves[i]
        return copy(piece(f, a, lo, n), piece(f, b, lo, n), gs.at[f, i], gr.at[f, i], to[f])

    def gstart(i):
        for f in (0, 1):
            start(gcopy(f, i))

    def gwait(i):
        for f in (0, 1):
            gcopy(f, i).wait_recv()

    def xcopy(k):
        return copy(
            u.at[pl.ds(same_row(k), ROWS), :], u.at[pl.ds(other_row(k), ROWS), :], cs.at[k], cr.at[k], core
        )

    for n, (d, slot) in enumerate(group):
        start(copy(labs.at[2 * PLACE[0] + 1], labs.at[slot], lsend.at[n], lrecv.at[n], d))
    for i in (0, 2, 4, 1, 3):
        start(gcopy(0, i))
    v[pl.ds(0, ROWS), :] = norm(txt_ref)
    for i in (0, 2, 4, 1, 3):
        start(gcopy(1, i))
    start(xcopy(0))

    scale = jnp.exp(jnp.full((8, 128), ls_ref[0], F32))
    c1 = scale[0:1, 0:1] * LOG2E
    c0 = jnp.full((1, 1), bias_ref[0] * LOG2E, F32)
    acc[...] = jnp.zeros_like(acc)

    gh = (g0, g1)
    one = jnp.minimum(im + 1, 1)

    def logits(row, h, n):
        rows = pl.ds(row, n)
        s = nt(u[rows, :], v[h * HALF : (h + 1) * HALF, :])
        l2 = s * c1 + c0
        e = jnp.exp2(l2)
        t = 1.0 + e
        r = pl.reciprocal(t, approx=True)
        lb = labb[rows, :]
        lbw = jnp.concatenate([lb] * 5 + [lb[:, :64]], axis=1)
        col = (lax.broadcasted_iota(jnp.int32, (n, HALF), 1) + h * HALF).astype(F32)
        pos = lbw == col
        gh[h][rows, :] = (r * jnp.where(pos, -1.0, e)).astype(BF16)
        t3 = t.reshape(n // 8, 8, HALF)
        p3 = jnp.where(pos, l2, 0.0).reshape(n // 8, 8, HALF)
        total = -jnp.sum(p3, axis=0)
        for a in range(0, n // 8, 8):
            w = t3[a]
            for b in range(a + 1, min(a + 8, n // 8)):
                w = w * t3[b]
            total = total + jnp.log2(w)
        acc[...] += total

    def logits_span(first, count, h):
        if count > 1:

            @pl.loop(0, count // 2 * one)
            def _(i):
                logits(pl.multiple_of((first + 2 * i) * 352, 16), h, 704)

        if count % 2:

            @pl.loop(0, one)
            def _(i):
                logits(pl.multiple_of((first + count - 1 + i) * 352, 16), h, 352)


    gwait(0)
    gstart(5)
    gstart(9)
    gstart(15)
    gwait(2)
    gstart(6)
    gstart(10)
    gstart(16)
    for n, (d, slot) in enumerate(group):
        copy(labs.at[2 * PLACE[0] + 1], labs.at[slot], lsend.at[n], lrecv.at[n], d).wait_recv()
    bases = []
    for dx, zz in ((0, z), (3, z), (1, z), (0, zt), (2, z), (3, zt), (1, zt), (2, zt)):
        i2, t2 = dev(dx=dx, zz=zz)
        bases.append((t2 * 8 + i2) * ROWS)
    for s in range(16):
        lab = labs[s]
        place = jnp.full((8, 128), -1, jnp.int32)
        for j, b in enumerate(bases):
            rel = lab - b
            place = jnp.where((rel >= 0) & (rel < ROWS), rel + ROWS * j, place)
        placef = place.astype(F32)
        first = jnp.broadcast_to(placef[0:1, :], (128, 128)).T
        second = jnp.broadcast_to(placef[1:2, :], (128, 128)).T
        labb[pl.ds(s * ROWS, 128), :] = first
        labb[pl.ds(s * ROWS + 128, 48), :] = second[0:48, :]

    gwait(4)
    gstart(7)
    gstart(8)
    gwait(1)
    gwait(3)
    for k in (1, 2, 3):
        start(xcopy(k))
    xcopy(0).wait_recv()
    logits_span(PLACE[0], 1, 0)
    gwait(5)
    gstart(11)
    gwait(6)
    gstart(12)
    for k in (1, 2, 3):
        xcopy(k).wait_recv()
    logits_span(PLACE[3], 2, 0)
    gwait(9)
    gstart(13)
    gwait(10)
    gstart(14)
    start(xcopy(4))
    logits_span(PLACE[2], 1, 0)
    xcopy(4).wait_recv()
    logits_span(PLACE[4], 1, 0)

    @pl.loop(0, 4 * one)
    def _(i):
        at = pl.multiple_of(i * 352, 16)
        pdu[pl.ds(at, 352), :] = nn(g0[pl.ds(same_row(4) + at, 352), :], v[0:HALF, :])

    @pl.loop(0, one)
    def _(_i):
        pdu[8 * ROWS :, :] = nn(g0[same_row(0) :, :], v[0:HALF, :])

    gwait(15)
    gwait(7)
    start(xcopy(5))
    gwait(16)
    gwait(8)
    start(xcopy(6))
    xcopy(5).wait_recv()
    logits_span(PLACE[5], 1, 0)
    for i in (11, 12, 13, 14):
        gwait(i)
    start(xcopy(7))
    logits_span(PLACE[4], 5, 1)
    xcopy(6).wait_recv()
    logits_span(PLACE[6], 1, 0)
    xcopy(7).wait_recv()
    logits_span(PLACE[7], 1, 0)
    logits_span(0, 3, 1)

    mine = jnp.broadcast_to(jnp.sum(acc[...]).reshape(1, 1), (8, 128))
    lossbuf[0] = mine
    y1 = 1 - 2 * (y % 2)
    x1 = 1 - 2 * (x % 2)
    pairs = (core, dev(dy=y1 + 4), dev(dy=4 - y1), dev(dx=x1 + 4), dev(dx=4 - x1), part[0], part[1])

    def pcopy(i):
        return copy(lossbuf.at[2 * i], lossbuf.at[2 * i + 1], ps.at[i], pr.at[i], pairs[i])

    def pnext(i):
        pcopy(i).wait_recv()
        lossbuf[2 * i + 2] = lossbuf[2 * i] + lossbuf[2 * i + 1]
        if i + 1 < 7:
            start(pcopy(i + 1))

    start(pcopy(0))

    rmoves = (
        (7, 0, CUTI, part),
        (7, CUTI, ROWS - CUTI, part),
        (5, SIDE, ROWS - SIDE, minus),
        (6, 0, ROWS - SIDE, plus),
        (4, 0, CUTI, minus),
        (4, CUTI, ROWS - CUTI, plus),
        (1, 0, CUTI, minus),
        (1, CUTI, ROWS - CUTI, minus),
        (2, 0, CUTI, plus),
        (2, CUTI, ROWS - CUTI, plus),
        (3, 0, ROWS, part),
        (5, 0, SIDE, part),
        (6, ROWS - SIDE, SIDE, part),
    )
    S7A, S7B, S5, S6, S4A, S4B, S1A, S1B, S2A, S2B, S3, S5Z, S6Z = range(13)

    def rcopy(f, i):
        k, lo, n, to = rmoves[i]
        sl = pl.ds(lo, n)
        return copy(stage.at[f, k - 1, sl, :], recv.at[f, k - 1, sl, :], rs.at[f, i], rr.at[f, i], to[f])

    def got(f, k, lo=0, n=ROWS):
        return recv[f, k - 1, lo : lo + n, :].astype(F32)

    def put(f, k, val, lo=0, n=ROWS):
        stage[f, k - 1, lo : lo + n, :] = val.astype(BF16)

    def ccopy(k):
        return copy(core_out.at[k], core_in.at[k], ccs.at[k], ccr.at[k], core)

    def du_block(k, nxt):
        @pl.loop(0, one)
        def _(_i):
            first = other_row(nxt) if k is None else same_row(k)
            n = ROWS if k is None or nxt is None else 352
            rows = pl.ds(first, n)
            d = nn(g1[rows, :], v[HALF:, :])
            if k in (None, 5, 6, 7):
                d = d + nn(g0[rows, :], v[0:HALF, :])
                if k is not None:
                    own[k - 5] = d[:ROWS]
            else:
                at = first - same_row(4)
                d = d + pdu[at : at + n, :]
                pdu[at : at + ROWS, :] = d[:ROWS]
            if nxt is not None:
                core_out[nxt] = d[n - ROWS :].astype(BF16)

        if nxt is not None:
            start(ccopy(nxt))

    def tcols(n):
        return slice(256 * n, min(256 * n + 256, D))

    tmoves = (
        (7, 0, ROWS, part),
        (5, SIDE, ROWS - SIDE, minus),
        (6, 0, ROWS - SIDE, plus),
        (3, 0, ROWS, part),
        (1, CUT, ROWS - CUT, minus),
        (2, 0, CUT, plus),
        (4, 0, CUT, minus),
        (4, CUT, ROWS - CUT, plus),
        (5, 0, SIDE, part),
        (6, ROWS - SIDE, SIDE, part),
        (1, 0, CUT, minus),
        (2, CUT, ROWS - CUT, plus),
    )
    T7, T5, T6, T3, T1B, T2A, T4A, T4B, T5Z, T6Z, T1A, T2B = range(12)

    def tcopy(i, n):
        k, lo, rows, to = tmoves[i]
        sl, cols = pl.ds(lo, rows), pl.ds(256 * n, min(256, D - 256 * n))
        return copy(
            stage.at[1, k - 1, sl, cols], recv.at[1, k - 1, sl, cols], ts.at[i, n], tr.at[i, n], to[1]
        )

    def twait(i):
        for n in range(5):
            tcopy(i, n).wait_recv()

    def dv_late(n, step=None):
        cols = tcols(n)

        @pl.loop(0, one)
        def _(_i):
            d = tn(g1[...], u[:, cols])
            dvt[:, cols] = d[0:ROWS]
            for k in (5, 6, 7):
                stage[1, k - 1, :, cols] = d[(k - 4) * ROWS : (k - 3) * ROWS].astype(BF16)

        if step is not None:
            pnext(step)
        for i in (T7, T5, T6, T5Z, T6Z):
            start(tcopy(i, n))

    def dv_early(n):
        cols = tcols(n)
        for i in (T5, T6):
            tcopy(i, n).wait_recv()

        @pl.loop(0, one)
        def _(_i):
            d = tn(g0[...], u[:, cols])
            dvf[0 : 3 * ROWS, cols] = d[0 : 3 * ROWS]
            stage[1, 0, CUT:, cols] = d[ROWS + CUT : 2 * ROWS].astype(BF16)
            stage[1, 1, 0:CUT, cols] = d[2 * ROWS : 2 * ROWS + CUT].astype(BF16)
            t = d[3 * ROWS :]
            lo, mid, hi = slice(0, SIDE), slice(SIDE, ROWS - SIDE), slice(ROWS - SIDE, ROWS)
            r5, r6 = recv.at[1, 4], recv.at[1, 5]
            stage[1, 2, lo, cols] = (t[lo] + r6[lo, cols].astype(F32)).astype(BF16)
            both = r5[mid, cols].astype(F32) + r6[mid, cols].astype(F32)
            stage[1, 2, mid, cols] = (t[mid] + both).astype(BF16)
            stage[1, 2, hi, cols] = (t[hi] + r5[hi, cols].astype(F32)).astype(BF16)

        for i in (T3, T1B, T2A):
            start(tcopy(i, n))

    def mine_of(k, lo=0, n=ROWS):
        if k >= 5:
            mine = own[k - 5, lo : lo + n, :]
        else:
            at = same_row(k) - same_row(4) + lo
            mine = pdu[at : at + n, :]
        return mine + core_in[k, lo : lo + n, :].astype(F32)

    du_block(None, 7)
    dv_late(0, 0)
    du_block(7, 5)
    ccopy(7).wait_recv()
    put(0, 7, mine_of(7))
    start(rcopy(0, S7A))
    start(rcopy(0, S7B))
    du_block(5, 6)
    ccopy(5).wait_recv()
    put(0, 5, mine_of(5))
    pnext(1)
    start(rcopy(0, S5))
    start(rcopy(0, S5Z))
    du_block(6, 4)
    ccopy(6).wait_recv()
    put(0, 6, mine_of(6))
    start(rcopy(0, S6))
    start(rcopy(0, S6Z))
    dv_late(1, 2)
    dv_late(2)
    dv_late(3)
    dv_late(4, 3)
    du_block(4, 3)

    ccopy(4).wait_recv()
    rcopy(0, S7A).wait_recv()
    put(0, 4, mine_of(4, 0, CUTI) + got(0, 7, 0, CUTI), 0, CUTI)
    start(rcopy(0, S4A))
    du_block(3, 1)
    rcopy(0, S7B).wait_recv()
    put(0, 4, mine_of(4, CUTI, ROWS - CUTI) + got(0, 7, CUTI, ROWS - CUTI), CUTI, ROWS - CUTI)
    start(rcopy(0, S4B))

    def text_four(n):
        cols = tcols(n)
        tcopy(T7, n).wait_recv()
        stage[1, 3, :, cols] = (dvt[:, cols] + recv[1, 6, :, cols].astype(F32)).astype(BF16)
        start(tcopy(T4A, n))
        start(tcopy(T4B, n))

    def text_last(n):
        cols = tcols(n)
        for i in (T4A, T4B, T5Z, T6Z):
            tcopy(i, n).wait_recv()

        def add(k, lo, hi, *more):
            t = dvf[k * ROWS + lo : k * ROWS + hi, cols]
            for j in more:
                t = t + recv[1, j - 1, lo:hi, cols].astype(F32)
            stage[1, k - 1, lo:hi, cols] = t.astype(BF16)

        add(1, 0, SIDE, 4, 5)
        add(1, SIDE, CUT, 4)
        start(tcopy(T1A, n))
        add(2, CUT, ROWS - SIDE, 4)
        add(2, ROWS - SIDE, ROWS, 4, 6)
        start(tcopy(T2B, n))

    text_four(0)
    text_four(1)
    dv_early(0)
    text_four(2)
    du_block(1, 2)
    ccopy(1).wait_recv()
    put(0, 1, mine_of(1, CUTI, ROWS - CUTI), CUTI, ROWS - CUTI)
    start(rcopy(0, S1B))
    text_four(3)
    du_block(2, 0)
    ccopy(2).wait_recv()
    put(0, 2, mine_of(2, 0, CUTI), 0, CUTI)
    start(rcopy(0, S2A))
    dv_early(1)
    text_four(4)
    ccopy(3).wait_recv()
    rcopy(0, S5).wait_recv()
    rcopy(0, S6).wait_recv()
    end = ROWS - SIDE
    put(0, 3, mine_of(3, 0, SIDE) + got(0, 6, 0, SIDE), 0, SIDE)
    mid = got(0, 5, SIDE, end - SIDE) + got(0, 6, SIDE, end - SIDE)
    put(0, 3, mine_of(3, SIDE, end - SIDE) + mid, SIDE, end - SIDE)
    put(0, 3, mine_of(3, end, SIDE) + got(0, 5, end, SIDE), end, SIDE)
    pnext(4)
    start(rcopy(0, S3))
    dv_early(2)
    dv_early(3)

    rcopy(0, S4A).wait_recv()
    rcopy(0, S5Z).wait_recv()
    first = mine_of(1, 0, SIDE) + got(0, 4, 0, SIDE) + got(0, 5, 0, SIDE)
    put(0, 1, first, 0, SIDE)
    put(0, 1, mine_of(1, SIDE, CUTI - SIDE) + got(0, 4, SIDE, CUTI - SIDE), SIDE, CUTI - SIDE)
    start(rcopy(0, S1A))
    rcopy(0, S4B).wait_recv()
    rcopy(0, S6Z).wait_recv()
    put(0, 2, mine_of(2, CUTI, end - CUTI) + got(0, 4, CUTI, end - CUTI), CUTI, end - CUTI)
    put(0, 2, mine_of(2, end, SIDE) + got(0, 4, end, SIDE) + got(0, 6, end, SIDE), end, SIDE)
    start(rcopy(0, S2B))
    text_last(0)
    text_last(1)
    text_last(2)
    dv_early(4)
    text_last(3)
    text_last(4)
    pnext(5)
    du_block(0, None)

    ccopy(0).wait_recv()

    def finish(f, ref, out, grad, lo, n):
        rows = ref[lo : lo + n, :].astype(F32)
        inv = lax.rsqrt(jnp.sum(rows * rows, axis=-1, keepdims=True) + EPS)
        unit = rows * inv
        grad = (grad + got(f, 1, lo, n) + got(f, 2, lo, n) + got(f, 3, lo, n)) * scale[0:1, 0:1]
        out[lo : lo + n, :] = (grad - unit * jnp.sum(unit * grad, axis=-1, keepdims=True)) * inv

    for i in (S1B, S2A, S3, S1A):
        rcopy(0, i).wait_recv()
    finish(0, img_ref, du_ref, mine_of(0, 0, CUTI), 0, CUTI)
    for i in (T3, T1B, T2A):
        twait(i)
    twait(T1A)
    finish(1, txt_ref, dv_ref, dvf[0:CUT, :], 0, CUT)
    rcopy(0, S2B).wait_recv()
    finish(0, img_ref, du_ref, mine_of(0, CUTI, ROWS - CUTI), CUTI, ROWS - CUTI)
    twait(T2B)
    finish(1, txt_ref, dv_ref, dvf[CUT:ROWS, :], CUT, ROWS - CUT)
    pnext(6)
    loss_ref[0] = jnp.max(lossbuf[14]) * (LN2 / BATCH)

    for cp in sent:
        cp.wait_send()


def fused(log_scale, bias, images, texts, labels):
    vm = pl.BlockSpec(memory_space=pltpu.VMEM)
    sm = pl.BlockSpec(memory_space=pltpu.SMEM)
    dma = pltpu.SemaphoreType.DMA
    block = pltpu.VMEM((ROWS, D), F32)
    return pl.pallas_call(
        kernel,
        out_shape=(block, block, jax.ShapeDtypeStruct((1,), F32)),
        in_specs=[sm, sm, vm, vm, vm],
        out_specs=(vm, vm, sm),
        scratch_shapes=[
            pltpu.VMEM((16 * ROWS, D), BF16),
            pltpu.VMEM((8 * ROWS, D), BF16),
            pltpu.VMEM((16 * ROWS, HALF), BF16),
            pltpu.VMEM((16 * ROWS, HALF), BF16),
            pltpu.VMEM((16, 8, 128), jnp.int32),
            pltpu.VMEM((16 * ROWS, 128), F32),
            pltpu.VMEM((8, HALF), F32),
            pltpu.VMEM((15, 8, 128), F32),
            pltpu.VMEM((HALF, D), F32),
            pltpu.VMEM((8, ROWS, D), BF16),
            pltpu.VMEM((8, ROWS, D), BF16),
            pltpu.VMEM((2, 7, ROWS, D), BF16),
            pltpu.VMEM((2, 7, ROWS, D), BF16),
            pltpu.VMEM((3, ROWS, D), F32),
            pltpu.VMEM((9 * ROWS, D), F32),
            pltpu.VMEM((ROWS, D), F32),
            dma((2, 17)), dma((2, 17)),
            dma((8,)), dma((8,)),
            dma((15,)), dma((15,)),
            dma((2, 13)), dma((2, 13)),
            dma((8,)), dma((8,)),
            dma((7,)), dma((7,)),
            dma((12, 5)), dma((12, 5)),
        ],
        compiler_params=pltpu.CompilerParams(
            collective_id=0, has_side_effects=True, vmem_limit_bytes=60 << 20
        ),
        name="contrastive",
    )(log_scale, bias, images, texts, labels)


def body(images, texts, match, log_scale, bias):
    du, dv, loss = fused(log_scale.reshape(1), bias.reshape(1), images, texts, match.reshape(1, ROWS))
    return (loss.reshape(()), du, dv)


def solution(mesh):
    in_specs = (P(("img", "txt"), None), P(("txt", "img"), None), P(("img", "txt")), P(), P())
    out_specs = (P(), P(("img", "txt"), None), P(("txt", "img"), None))
    return jax.shard_map(body, mesh=mesh, in_specs=in_specs, out_specs=out_specs, check_vma=False)
```
